768 devices in a mesh: dp: 3 (over z_lo), mp: 64 (over z_hi, y, core), inner: 4 (over x).
Axes of the slice: x: 4, y: 8, z: 12 (z_hi: 4, z_lo: 3; z = z_hi * 3 + z_lo), core: 2. Of those that a mesh axis runs over, the one named last changes fastest.
Arguments:
- grads: bfloat16 [3, 3, 256, 512, 512], P('dp', None, None, 'mp', 'inner'), may hold values from -33 to 33, as said below
- table: int32 [3, 256, 1], P('dp'), may hold values from 0 to 63; in each aligned block of 256 rows (0 to 255, 256 to 511, ..., all dimensions but the last counted through in order) at most 8 rows name the same one
- left_root: bfloat16 [3, 64, 8, 512, 512], P('dp', 'mp'), may hold values from -1 to 9, as said below
- right_root: bfloat16 [3, 64, 8, 512, 512], P('dp', 'mp', None, None, 'inner'), may hold values from -1 to 9, as said below
Outputs:
- directions: bfloat16 [3, 256, 512, 512], P('dp', None, 'mp', 'inner')
The draws below stay inside these ranges and needn't reach their ends.
Inputs may be any that keep to these rules, and one draw needn't show every extreme that they name: `table`: in each span no owner holds more than 8 blocks, and in some span one owner holds exactly 8. `grads`: each replica's gradient block. `left_root`: slot c of owner o in span d holds the factor of the c-th block of span d that the table gives to o; slots beyond an owner's count are not read. `right_root`: laid out in slots as left_root.
All inputs are finite; a program needn't handle non-finite values.
Results may differ from the reference program's by a relative error of at most 0.014.
Values may be sent and summed in bfloat16 or wider, within the bound.
No kernel may reach another device: no remote copies, remote signals or barrier semaphores. Data moves between devices by JAX's collectives and lax.ppermute only.
A program may use at most 32 MiB of HBM per device.

```python
import math
import jax
import jax.numpy as jnp
import numpy as np
from jax import lax

B = 512
CAP = 8
GROUP = 256
N_DP = 3
N_MP = 64


def symmetric_factor(key, low, high):
    shape = (N_DP, N_MP, CAP, B, B)
    first, second = jax.random.split(key)
    diagonal = jnp.exp(jax.random.uniform(first, (N_DP, N_MP, CAP, 1, B), jnp.float32, math.log(low), math.log(high)))
    noise = jnp.clip(jax.random.normal(second, shape, jnp.float32), -4.0, 4.0)
    mixed = (noise + jnp.swapaxes(noise, -1, -2)) * (0.45 / math.sqrt(2.0 * B))
    identity = jnp.arange(B)[:, None] == jnp.arange(B)[None, :]
    return (mixed + jnp.where(identity, diagonal, 0.0)).astype(jnp.bfloat16)


def draw_left_root(key, part):
    key = jax.random.fold_in(key, 2)
    return symmetric_factor(key, 1.0, 4.0)


def draw_right_root(key, part):
    key = jax.random.fold_in(key, 3)
    return symmetric_factor(key, 1.0, 4.0)


def draw_grads(key, part):
    key = jax.random.fold_in(key, 1)
    keys = jax.random.split(key, 3)
    shape = (N_DP, N_DP, GROUP, B, B)
    low, high = (0.3, 3.0)
    row_scale = jnp.exp(jax.random.uniform(keys[0], (1, N_DP, GROUP, B, 1), jnp.float32, math.log(low), math.log(high)))
    col_scale = jnp.exp(jax.random.uniform(keys[1], (1, N_DP, GROUP, 1, B), jnp.float32, math.log(low), math.log(high)))
    values = 0.35 * jnp.clip(jax.random.normal(keys[2], shape, jnp.float32), -4.0, 4.0)
    return (row_scale * col_scale * values).astype(jnp.bfloat16)


def shared_out(rng, own, number, rows, count, top, most, lean):
    ranking = jax.random.permutation(rng, count)
    crowded, usual = portions_of(count, rows * top, most, lean, True), portions_of(count, rows * top, most, lean, False)
    places = jnp.arange(count)

    def named(lengths, turn):
        used = int((lengths > 0).sum())
        fixed = max(1, used // 4)
        moved = fixed + (places - fixed + turn * (used - fixed)) % max(1, count - fixed)
        return jnp.zeros((count,), jnp.int32).at[ranking[jnp.where(places < fixed, places, moved)]].set(jnp.asarray(lengths, jnp.int32))

    lengths = jnp.where(number % 4 == 0, named(crowded, number // 4), named(usual, number - number // 4 - 1))
    mixed = jax.random.permutation(jax.random.fold_in(own, 3), count)
    giver, taker = mixed[0:count // 2 * 2:2], mixed[1:count // 2 * 2:2]
    margin = jnp.minimum(lengths[giver] - 1, most - lengths[taker]) // 2
    margin = jnp.where((giver == ranking[0]) | (taker == ranking[0]) | (lengths[taker] == 0), 0, jnp.maximum(margin, 0))
    moved = jax.random.randint(jax.random.fold_in(own, 4), (count // 2,), 0, 1 << 20) % (margin + 1)
    lengths = lengths.at[giver].add(-moved).at[taker].add(moved)
    items = jnp.searchsorted(jnp.cumsum(lengths), jnp.arange(rows * top), side="right").astype(jnp.int32)
    table = items.reshape(top, rows).T
    table = table[jax.random.permutation(jax.random.fold_in(own, 1), rows)]
    turn = jax.random.randint(jax.random.fold_in(own, 2), (rows, 1), 0, top)
    return jnp.take_along_axis(table, (jnp.arange(top)[None, :] + turn) % top, axis=1)


def portions_of(number_of, total, reach, lean, full):
    weights = [(1 << 20) // math.isqrt(grade ** lean) + 1 for grade in range(1, number_of + 1)]
    largest = reach if full else min(reach, max(-(-total // number_of), total * weights[0] // sum(weights)))
    least = 1 if total - largest >= number_of - 1 else 0
    given, surplus = [largest] + [least] * (number_of - 1), total - largest - least * (number_of - 1)
    while surplus > 0:
        candidates = [i for i in range(1, number_of) if given[i] < largest] or [i for i in range(1, number_of) if given[i] < reach]
        pool, budget = sum([weights[i] for i in candidates]), surplus
        for i in candidates:
            more = min(reach - given[i], max(1, budget * weights[i] // pool), surplus)
            given[i] = given[i] + more
            surplus = surplus - more
    return np.array(given)


def setup_inputs(seed: int = 0) -> dict:
    arg_keys = jax.random.split(jax.random.key(seed), 5)
    grads = draw_grads(jax.random.fold_in(arg_keys[4], 71), 0)
    table_keys = jax.random.split(jax.random.fold_in(arg_keys[1], 1), N_DP * GROUP // GROUP)
    table_turns = jax.random.permutation(jax.random.fold_in(arg_keys[1], 3), N_DP * GROUP // GROUP)
    table = jax.vmap(lambda own, number: shared_out(jax.random.fold_in(arg_keys[1], 2), own, number, GROUP, N_MP, 1, CAP, 2))(table_keys, table_turns).reshape((N_DP, GROUP, 1))
    left_root = draw_left_root(jax.random.fold_in(arg_keys[4], 71), 0)
    right_root = draw_right_root(jax.random.fold_in(arg_keys[4], 71), 0)
    return dict(grads=grads, table=table, left_root=left_root, right_root=right_root)


def reference(grads, table, left_root, right_root):
    owner = table[:, :, 0].astype(jnp.int32)
    owners = jnp.arange(N_MP, dtype=jnp.int32)
    onehot = (owner[:, :, None] == owners[None, None, :]).astype(jnp.int32)
    rank = lax.optimization_barrier(jnp.sum((jnp.cumsum(onehot, axis=1) - onehot) * onehot, axis=2)).astype(jnp.int32)
    span = jnp.repeat(jnp.arange(N_DP, dtype=jnp.int32), GROUP)
    within = jnp.tile(jnp.arange(GROUP, dtype=jnp.int32), N_DP)

    def one_block(index):
        span_id = index[0]
        block_id = index[1]
        holder = owner[span_id, block_id]
        place = rank[span_id, block_id]
        summed = lax.optimization_barrier(jnp.sum(grads[:, span_id, block_id].astype(jnp.float32), axis=0))
        gradient = summed.astype(jnp.bfloat16)
        left_product = jnp.dot(left_root[span_id, holder, place], gradient, preferred_element_type=jnp.float32).astype(jnp.bfloat16)
        preconditioned = jnp.dot(left_product, right_root[span_id, holder, place], preferred_element_type=jnp.float32)
        grad_square = jnp.sum(jnp.square(gradient.astype(jnp.float32)))
        pre_square = jnp.sum(jnp.square(preconditioned))
        return (preconditioned * jnp.sqrt(grad_square / (pre_square + 1e-06))).astype(jnp.bfloat16)
    result = lax.map(one_block, jnp.stack([span, within], axis=1))
    return result.reshape(N_DP, GROUP, B, B)
```

```python
import functools

import jax
import jax.numpy as jnp
from jax import lax
from jax.experimental import pallas as pl
from jax.experimental.pallas import tpu as pltpu
from jax.sharding import PartitionSpec as P

GROUP_AXES = ("mp", "inner")


def ring(size, step):
    return [(i, (i + step) % size) for i in range(size)]


def grafted(received_ref, left_ref, right_ref, out_ref):
    pieces, parts, pair_rows, lanes = received_ref.shape
    held = left_ref.shape[0]
    row_len = pair_rows // held
    directions = []
    for slot in range(held):
        rows = slice(slot * row_len, (slot + 1) * row_len)
        gradient = jnp.concatenate(
            [
                received_ref[:, part]
                .astype(jnp.float32)[:, rows]
                .reshape(pieces * row_len, lanes)
                for part in range(parts)
            ],
            axis=1,
        )
        left = jnp.dot(
            left_ref[slot], gradient.astype(jnp.bfloat16), preferred_element_type=jnp.float32
        ).astype(jnp.bfloat16)
        right = jnp.concatenate([right_ref[part, slot] for part in range(parts)], axis=1)
        product = jnp.dot(left, right, preferred_element_type=jnp.float32)
        grad_square = jnp.sum(jnp.square(gradient))
        pre_square = jnp.sum(jnp.square(product))
        factor = jnp.sqrt(jnp.full((1, lanes), grad_square / (pre_square + 1e-06), jnp.float32))
        directions.append(product * factor[:, :1])
    for part in range(parts):
        columns = slice(part * lanes, (part + 1) * lanes)
        out_ref[:, part] = jnp.concatenate(
            [each[:, columns].reshape(pieces, row_len, lanes) for each in directions], axis=1
        ).astype(jnp.bfloat16)


def shards(grads, table, left_root, right_root):
    replicas = lax.axis_size("dp")
    owners_count = lax.axis_size("mp")
    parts = lax.axis_size("inner")
    capacity = left_root.shape[2]
    held = capacity // parts
    _, _, group_len, row_len, col_len = grads.shape
    slot_total = owners_count * capacity
    me = lax.axis_index("dp")
    inner = lax.axis_index("inner")

    terms = [lax.dynamic_index_in_dim(grads[0], me, 0, keepdims=False)]
    for step in range(1, replicas):
        other = lax.rem(me + step, replicas)
        sent = lax.dynamic_index_in_dim(grads[0], other, 0, keepdims=False)
        terms.append(lax.ppermute(sent, "dp", ring(replicas, step)))

    right = lax.all_to_all(
        right_root[0, 0].reshape(parts, held, *right_root.shape[3:]), "inner", 0, 0, tiled=True
    )
    left = lax.dynamic_slice_in_dim(left_root[0, 0], inner * held, held, 0)

    owner = table[0, :, 0]
    onehot = (owner[:, None] == jnp.arange(owners_count, dtype=jnp.int32)[None, :]).astype(
        jnp.int32
    )
    rank = jnp.sum((jnp.cumsum(onehot, axis=0) - onehot) * onehot, axis=1)
    target = owner * capacity + rank
    slots = jnp.arange(slot_total, dtype=jnp.int32)
    pick_send = (target[None, :] == slots[:, None]).astype(jnp.bfloat16)
    pick_back = (target[:, None] == slots[None, :]).astype(jnp.bfloat16)

    summed = functools.reduce(jnp.add, [term.astype(jnp.float32) for term in terms])
    gradient = summed.astype(jnp.bfloat16)
    outgoing = jnp.dot(
        pick_send,
        gradient.reshape(group_len, row_len * col_len),
        preferred_element_type=jnp.float32,
    ).astype(jnp.bfloat16)
    outgoing = outgoing.reshape(owners_count * parts, held * row_len, col_len)
    received = lax.all_to_all(outgoing, GROUP_AXES, 0, 0, tiled=True)
    received = received.reshape(owners_count, parts, held * row_len, col_len)
    direction = pl.pallas_call(
        grafted,
        out_shape=jax.ShapeDtypeStruct(received.shape, jnp.bfloat16),
        compiler_params=pltpu.CompilerParams(vmem_limit_bytes=40 * 1024 * 1024),
    )(received, left, right)
    returned = lax.all_to_all(
        direction.reshape(owners_count * parts, held * row_len, col_len),
        GROUP_AXES,
        0,
        0,
        tiled=True,
    )
    gathered = jnp.dot(
        pick_back,
        returned.reshape(slot_total, row_len * col_len),
        preferred_element_type=jnp.float32,
    )
    return gathered.astype(jnp.bfloat16).reshape(1, group_len, row_len, col_len)


def solution(mesh):
    placed = (
        P("dp", None, None, "mp", "inner"),
        P("dp", None, None),
        P("dp", "mp", None, None, None),
        P("dp", "mp", None, None, "inner"),
    )
    return jax.shard_map(
        shards, mesh=mesh, in_specs=placed, out_specs=P("dp", None, "mp", "inner"), check_vma=False
    )
```

```python
import jax
import jax.numpy as jnp
from jax import lax
from jax.experimental import pallas as pl
from jax.experimental.pallas import tpu as pltpu
from jax.sharding import PartitionSpec as P

GROUP_AXES = ("mp", "inner")
UNROLL = 8
VMEM_BYTES = 40 * 1024 * 1024


def ring(size, step):
    return [(i, (i + step) % size) for i in range(size)]


def whole(shape):
    return pl.BlockSpec(shape, lambda *_: (0,) * len(shape))


def picked(source_ref, span_ref, own_ref, *rest):
    *terms, out_ref, total = rest
    summed = own_ref[0].astype(jnp.float32)
    for term in terms:
        summed = summed + term[...].astype(jnp.float32)
    total[...] = summed.astype(jnp.bfloat16)
    copied(source_ref, total, out_ref)


def copied(place_ref, from_ref, to_ref):
    def step(turn, carry):
        for offset in range(UNROLL):
            at = turn * UNROLL + offset
            to_ref[at] = from_ref[place_ref[at]]
        return carry

    lax.fori_loop(0, to_ref.shape[0] // UNROLL, step, 0)


def grafted(received_ref, left_ref, right_ref, out_ref):
    pieces, parts, held, row_len, lanes = received_ref.shape
    for slot in range(held):
        gradient = jnp.concatenate(
            [
                received_ref[:, part, slot]
                .astype(jnp.float32)
                .reshape(pieces * row_len, lanes)
                for part in range(parts)
            ],
            axis=1,
        )
        left = jnp.dot(
            left_ref[slot], gradient.astype(jnp.bfloat16), preferred_element_type=jnp.float32
        ).astype(jnp.bfloat16)
        right = jnp.concatenate([right_ref[part, slot] for part in range(parts)], axis=1)
        product = jnp.dot(left, right, preferred_element_type=jnp.float32)
        grad_square = jnp.sum(jnp.square(gradient))
        pre_square = jnp.sum(jnp.square(product))
        factor = jnp.sqrt(jnp.full((1, lanes), grad_square / (pre_square + 1e-06), jnp.float32))
        direction = product * factor[:, :1]
        for part in range(parts):
            out_ref[:, part, slot] = (
                direction[:, part * lanes : (part + 1) * lanes]
                .reshape(pieces, row_len, lanes)
                .astype(jnp.bfloat16)
            )


def shards(grads, table, left_root, right_root):
    replicas = lax.axis_size("dp")
    owners_count = lax.axis_size("mp")
    parts = lax.axis_size("inner")
    capacity = left_root.shape[2]
    held = capacity // parts
    _, _, group_len, row_len, col_len = grads.shape
    slot_total = owners_count * capacity
    me = lax.axis_index("dp")
    inner = lax.axis_index("inner")
    params = pltpu.CompilerParams(vmem_limit_bytes=VMEM_BYTES)

    terms = []
    for step in range(1, replicas):
        other = lax.rem(me + step, replicas)
        sent = lax.dynamic_index_in_dim(grads[0], other, 0, keepdims=False)
        terms.append(lax.ppermute(sent, "dp", ring(replicas, step)))

    owner = table[0, :, 0]
    onehot = (owner[:, None] == jnp.arange(owners_count, dtype=jnp.int32)[None, :]).astype(
        jnp.int32
    )
    rank = jnp.sum((jnp.cumsum(onehot, axis=0) - onehot) * onehot, axis=1)
    target = owner * capacity + rank
    slots = jnp.arange(slot_total, dtype=jnp.int32)
    blocks = jnp.arange(group_len, dtype=jnp.int32)
    source = jnp.sum(
        jnp.where(target[None, :] == slots[:, None], blocks[None, :], 0), axis=1
    ).astype(jnp.int32)

    right = lax.all_to_all(
        right_root[0, 0].reshape(parts, held, *right_root.shape[3:]), "inner", 0, 0, tiled=True
    )
    left = lax.dynamic_slice_in_dim(left_root[0, 0], inner * held, held, 0)
    source, left, right = lax.optimization_barrier((source, left, right))

    piece = (group_len, row_len, col_len)
    sending = (slot_total, row_len, col_len)
    outgoing = pl.pallas_call(
        picked,
        grid_spec=pltpu.PrefetchScalarGridSpec(
            num_scalar_prefetch=2,
            grid=(1,),
            in_specs=[pl.BlockSpec((1, *piece), lambda _, source, span: (span[0], 0, 0, 0))]
            + [whole(piece)] * (replicas - 1),
            out_specs=whole(sending),
            scratch_shapes=[pltpu.VMEM(piece, jnp.bfloat16)],
        ),
        out_shape=jax.ShapeDtypeStruct(sending, jnp.bfloat16),
        compiler_params=params,
    )(source, jnp.full((1,), me, jnp.int32), grads[0], *terms)
    outgoing, left, right = lax.optimization_barrier((outgoing, left, right))
    received = lax.all_to_all(outgoing, GROUP_AXES, 0, 0, tiled=True)
    shape = (owners_count, parts, held, row_len, col_len)
    direction = pl.pallas_call(
        grafted,
        out_shape=jax.ShapeDtypeStruct(shape, jnp.bfloat16),
        compiler_params=params,
    )(received.reshape(shape), left, right)
    returned = lax.all_to_all(direction.reshape(sending), GROUP_AXES, 0, 0, tiled=True)
    result = pl.pallas_call(
        copied,
        grid_spec=pltpu.PrefetchScalarGridSpec(
            num_scalar_prefetch=1,
            grid=(1,),
            in_specs=[whole(sending)],
            out_specs=whole(piece),
        ),
        out_shape=jax.ShapeDtypeStruct(piece, jnp.bfloat16),
        compiler_params=params,
    )(target, returned)
    return result[None]


def solution(mesh):
    placed = (
        P("dp", None, None, "mp", "inner"),
        P("dp", None, None),
        P("dp", "mp", None, None, None),
        P("dp", "mp", None, None, "inner"),
    )
    return jax.shard_map(
        shards, mesh=mesh, in_specs=placed, out_specs=P("dp", None, "mp", "inner"), check_vma=False
    )
```

```python
import jax
import jax.numpy as jnp
from jax import lax
from jax.experimental import pallas as pl
from jax.experimental.pallas import tpu as pltpu
from jax.sharding import PartitionSpec as P

GROUP_AXES = ("mp", "inner")
UNROLL = 8
MIB = 1024 * 1024
IN_SMEM = pl.BlockSpec(memory_space=pltpu.SMEM)
IN_VMEM = pl.BlockSpec(memory_space=pltpu.VMEM)
IN_ANY = pl.BlockSpec(memory_space=pl.ANY)


def ring(size, step):
    return [(i, (i + step) % size) for i in range(size)]


def picked(source_ref, *rest):
    *terms, out_ref, total = rest
    summed = terms[0][...].astype(jnp.float32)
    for term in terms[1:]:
        summed = summed + term[...].astype(jnp.float32)
    total[...] = summed.astype(jnp.bfloat16)
    copied(source_ref, total, out_ref)


def copied(place_ref, from_ref, to_ref):
    def step(turn, carry):
        for offset in range(UNROLL):
            at = turn * UNROLL + offset
            to_ref[at] = from_ref[place_ref[at]]
        return carry

    lax.fori_loop(0, to_ref.shape[0] // UNROLL, step, 0)


def grafted(place_ref, received_ref, left_ref, right_ref, out_ref, left_held, right_held, ready):
    pieces, parts, pair_rows, lanes = received_ref.shape
    held = left_held.shape[0]
    row_len = pair_rows // held
    first = place_ref[0] * held
    left_copy = pltpu.make_async_copy(left_ref.at[pl.ds(first, held)], left_held, ready.at[0])
    right_copy = pltpu.make_async_copy(
        right_ref.at[:, pl.ds(first, held)], right_held, ready.at[1]
    )
    left_copy.start()
    right_copy.start()
    gradients = []
    for slot in range(held):
        rows = slice(slot * row_len, (slot + 1) * row_len)
        gradients.append(
            jnp.concatenate(
                [
                    received_ref[:, part]
                    .astype(jnp.float32)[:, rows]
                    .reshape(pieces * row_len, lanes)
                    for part in range(parts)
                ],
                axis=1,
            )
        )
    left_copy.wait()
    right_copy.wait()
    directions = []
    for slot, gradient in enumerate(gradients):
        left = jnp.dot(
            left_held[slot], gradient.astype(jnp.bfloat16), preferred_element_type=jnp.float32
        ).astype(jnp.bfloat16)
        right = jnp.concatenate([right_held[part, slot] for part in range(parts)], axis=1)
        product = jnp.dot(left, right, preferred_element_type=jnp.float32)
        grad_square = jnp.sum(jnp.square(gradient))
        pre_square = jnp.sum(jnp.square(product))
        factor = jnp.sqrt(jnp.full((1, lanes), grad_square / (pre_square + 1e-06), jnp.float32))
        directions.append(product * factor[:, :1])
    for part in range(parts):
        columns = slice(part * lanes, (part + 1) * lanes)
        out_ref[:, part] = jnp.concatenate(
            [each[:, columns].reshape(pieces, row_len, lanes) for each in directions], axis=1
        ).astype(jnp.bfloat16)


def shards(grads, table, left_root, right_root):
    replicas = lax.axis_size("dp")
    owners_count = lax.axis_size("mp")
    parts = lax.axis_size("inner")
    capacity = left_root.shape[2]
    held = capacity // parts
    _, _, group_len, row_len, col_len = grads.shape
    slot_total = owners_count * capacity
    me = lax.axis_index("dp")
    inner = lax.axis_index("inner")
    params = pltpu.CompilerParams(vmem_limit_bytes=32 * MIB)

    terms = [lax.dynamic_index_in_dim(grads[0], me, 0, keepdims=False)]
    for step in range(1, replicas):
        other = lax.rem(me + step, replicas)
        sent = lax.dynamic_index_in_dim(grads[0], other, 0, keepdims=False)
        terms.append(lax.ppermute(sent, "dp", ring(replicas, step)))
    right = lax.all_gather(right_root[0, 0], "inner", axis=0, tiled=False)

    owner = table[0, :, 0]
    onehot = (owner[:, None] == jnp.arange(owners_count, dtype=jnp.int32)[None, :]).astype(
        jnp.int32
    )
    rank = jnp.sum((jnp.cumsum(onehot, axis=0) - onehot) * onehot, axis=1)
    target = owner * capacity + rank
    slots = jnp.arange(slot_total, dtype=jnp.int32)
    blocks = jnp.arange(group_len, dtype=jnp.int32)
    source = jnp.sum(
        jnp.where(target[None, :] == slots[:, None], blocks[None, :], 0), axis=1
    ).astype(jnp.int32)

    piece = (group_len, row_len, col_len)
    sending = (slot_total, row_len, col_len)
    paired = (owners_count * parts, held * row_len, col_len)
    outgoing = pl.pallas_call(
        picked,
        in_specs=[IN_SMEM] + [IN_VMEM] * replicas,
        out_specs=IN_VMEM,
        out_shape=jax.ShapeDtypeStruct(sending, jnp.bfloat16),
        scratch_shapes=[pltpu.VMEM(piece, jnp.bfloat16)],
        compiler_params=params,
    )(source, *terms)
    received = lax.all_to_all(outgoing.reshape(paired), GROUP_AXES, 0, 0, tiled=True)
    shape = (owners_count, parts, held * row_len, col_len)
    direction = pl.pallas_call(
        grafted,
        in_specs=[IN_SMEM, IN_VMEM, IN_ANY, IN_ANY],
        out_specs=IN_VMEM,
        out_shape=jax.ShapeDtypeStruct(shape, jnp.bfloat16),
        scratch_shapes=[
            pltpu.VMEM((held, *left_root.shape[3:]), jnp.bfloat16),
            pltpu.VMEM((parts, held, *right_root.shape[3:]), jnp.bfloat16),
            pltpu.SemaphoreType.DMA((2,)),
        ],
        compiler_params=pltpu.CompilerParams(vmem_limit_bytes=50 * MIB),
    )(jnp.full((1,), inner, jnp.int32), received.reshape(shape), left_root[0, 0], right)
    returned = lax.all_to_all(direction.reshape(paired), GROUP_AXES, 0, 0, tiled=True)
    result = pl.pallas_call(
        copied,
        in_specs=[IN_SMEM, IN_VMEM],
        out_specs=IN_VMEM,
        out_shape=jax.ShapeDtypeStruct(piece, jnp.bfloat16),
        compiler_params=params,
    )(target, returned.reshape(sending))
    return result[None]


def solution(mesh):
    placed = (
        P("dp", None, None, "mp", "inner"),
        P("dp", None, None),
        P("dp", "mp", None, None, None),
        P("dp", "mp", None, None, "inner"),
    )
    return jax.shard_map(
        shards, mesh=mesh, in_specs=placed, out_specs=P("dp", None, "mp", "inner"), check_vma=False
    )
```

```python
import jax
import jax.numpy as jnp
from jax import lax
from jax.experimental import pallas as pl
from jax.experimental.pallas import tpu as pltpu
from jax.sharding import PartitionSpec as P

GROUP_AXES = ("mp", "inner")
UNROLL = 16
MIB = 1024 * 1024
IN_SMEM = pl.BlockSpec(memory_space=pltpu.SMEM)
IN_VMEM = pl.BlockSpec(memory_space=pltpu.VMEM)


def ring(size, step):
    return [(i, (i + step) % size) for i in range(size)]


def picked(source_ref, *rest):
    *terms, out_ref, total = rest
    summed = terms[0][...].astype(jnp.float32)
    for term in terms[1:]:
        summed = summed + term[...].astype(jnp.float32)
    total[...] = summed.astype(jnp.bfloat16)
    copied(source_ref, total, out_ref)


def copied(place_ref, from_ref, to_ref):
    def step(turn, carry):
        for offset in range(UNROLL):
            at = turn * UNROLL + offset
            to_ref[at] = from_ref[place_ref[at]]
        return carry

    lax.fori_loop(0, to_ref.shape[0] // UNROLL, step, 0)


def grafted(received_ref, left_ref, right_ref, out_ref):
    pieces, parts, pair_rows, lanes = received_ref.shape
    held = left_ref.shape[0]
    row_len = pair_rows // held
    directions = []
    for slot in range(held):
        rows = slice(slot * row_len, (slot + 1) * row_len)
        gradient = jnp.concatenate(
            [
                received_ref[:, part]
                .astype(jnp.float32)[:, rows]
                .reshape(pieces * row_len, lanes)
                for part in range(parts)
            ],
            axis=1,
        )
        left = jnp.dot(
            left_ref[slot], gradient.astype(jnp.bfloat16), preferred_element_type=jnp.float32
        ).astype(jnp.bfloat16)
        right = jnp.concatenate([right_ref[part, slot] for part in range(parts)], axis=1)
        product = jnp.dot(left, right, preferred_element_type=jnp.float32)
        grad_square = jnp.sum(jnp.square(gradient))
        pre_square = jnp.sum(jnp.square(product))
        factor = jnp.sqrt(jnp.full((1, lanes), grad_square / (pre_square + 1e-06), jnp.float32))
        directions.append(product * factor[:, :1])
    for part in range(parts):
        columns = slice(part * lanes, (part + 1) * lanes)
        out_ref[:, part] = jnp.concatenate(
            [each[:, columns].reshape(pieces, row_len, lanes) for each in directions], axis=1
        ).astype(jnp.bfloat16)


def shards(grads, table, left_root, right_root):
    replicas = lax.axis_size("dp")
    owners_count = lax.axis_size("mp")
    parts = lax.axis_size("inner")
    capacity = left_root.shape[2]
    held = capacity // parts
    _, _, group_len, row_len, col_len = grads.shape
    slot_total = owners_count * capacity
    me = lax.axis_index("dp")
    inner = lax.axis_index("inner")
    params = pltpu.CompilerParams(vmem_limit_bytes=32 * MIB)

    terms = [lax.dynamic_index_in_dim(grads[0], me, 0, keepdims=False)]
    for step in range(1, replicas):
        other = lax.rem(me + step, replicas)
        sent = lax.dynamic_index_in_dim(grads[0], other, 0, keepdims=False)
        terms.append(lax.ppermute(sent, "dp", ring(replicas, step)))
    right = lax.all_to_all(
        right_root[0, 0].reshape(parts, held, *right_root.shape[3:]), "inner", 0, 0, tiled=True
    )

    left = lax.dynamic_slice_in_dim(left_root[0, 0], inner * held, held, 0)

    owner = table[0, :, 0]
    onehot = (owner[:, None] == jnp.arange(owners_count, dtype=jnp.int32)[None, :]).astype(
        jnp.int32
    )
    rank = jnp.sum((jnp.cumsum(onehot, axis=0) - onehot) * onehot, axis=1)
    target = owner * capacity + rank
    slots = jnp.arange(slot_total, dtype=jnp.int32)
    blocks = jnp.arange(group_len, dtype=jnp.int32)
    source = jnp.sum(
        jnp.where(target[None, :] == slots[:, None], blocks[None, :], 0), axis=1
    ).astype(jnp.int32)

    piece = (group_len, row_len, col_len)
    sending = (slot_total, row_len, col_len)
    paired = (owners_count * parts, held * row_len, col_len)
    outgoing = pl.pallas_call(
        picked,
        in_specs=[IN_SMEM] + [IN_VMEM] * replicas,
        out_specs=IN_VMEM,
        out_shape=jax.ShapeDtypeStruct(sending, jnp.bfloat16),
        scratch_shapes=[pltpu.VMEM(piece, jnp.bfloat16)],
        compiler_params=params,
    )(source, *terms)
    received = lax.all_to_all(outgoing.reshape(paired), GROUP_AXES, 0, 0, tiled=True)
    shape = (owners_count, parts, held * row_len, col_len)
    direction = pl.pallas_call(
        grafted,
        in_specs=[IN_VMEM] * 3,
        out_specs=IN_VMEM,
        out_shape=jax.ShapeDtypeStruct(shape, jnp.bfloat16),
        compiler_params=params,
    )(received.reshape(shape), left, right)
    returned = lax.all_to_all(direction.reshape(paired), GROUP_AXES, 0, 0, tiled=True)
    result = pl.pallas_call(
        copied,
        in_specs=[IN_SMEM, IN_VMEM],
        out_specs=IN_VMEM,
        out_shape=jax.ShapeDtypeStruct(piece, jnp.bfloat16),
        compiler_params=params,
    )(target, returned.reshape(sending))
    return result[None]


def solution(mesh):
    placed = (
        P("dp", None, None, "mp", "inner"),
        P("dp", None, None),
        P("dp", "mp", None, None, None),
        P("dp", "mp", None, None, "inner"),
    )
    return jax.shard_map(
        shards, mesh=mesh, in_specs=placed, out_specs=P("dp", None, "mp", "inner"), check_vma=False
    )
```

```python
import jax
import jax.numpy as jnp
from jax import lax
from jax.experimental import pallas as pl
from jax.experimental.pallas import tpu as pltpu
from jax.sharding import PartitionSpec as P

GROUP_AXES = ("mp", "inner")
UNROLL = 16
MIB = 1024 * 1024
IN_SMEM = pl.BlockSpec(memory_space=pltpu.SMEM)
IN_VMEM = pl.BlockSpec(memory_space=pltpu.VMEM)
IN_ANY = pl.BlockSpec(memory_space=pl.ANY)


def ring(size, step):
    return [(i, (i + step) % size) for i in range(size)]


def spans(grads_ref, *rest):
    *out_refs, ready = rest
    me = lax.axis_index("dp")
    copies = []
    for step, out_ref in enumerate(out_refs):
        span = lax.rem(me + step, len(out_refs))
        copies.append(pltpu.make_async_copy(grads_ref.at[span], out_ref, ready.at[step]))
    for copy in copies:
        copy.start()
    for copy in copies:
        copy.wait()


def summed_into_slots(target_ref, *rest):
    *terms, out_ref = rest
    out_ref[...] = jnp.zeros_like(out_ref)

    def step(turn, carry):
        for offset in range(UNROLL):
            block = turn * UNROLL + offset
            summed = terms[0][block].astype(jnp.float32)
            for term in terms[1:]:
                summed = summed + term[block].astype(jnp.float32)
            out_ref[target_ref[block]] = summed.astype(jnp.bfloat16)
        return carry

    lax.fori_loop(0, terms[0].shape[0] // UNROLL, step, 0)


def copied(place_ref, from_ref, to_ref):
    def step(turn, carry):
        for offset in range(UNROLL):
            at = turn * UNROLL + offset
            to_ref[at] = from_ref[place_ref[at]]
        return carry

    lax.fori_loop(0, to_ref.shape[0] // UNROLL, step, 0)


def grafted(received_ref, left_ref, right_ref, out_ref):
    pieces, parts, pair_rows, lanes = received_ref.shape
    held = left_ref.shape[0]
    row_len = pair_rows // held
    directions = []
    for slot in range(held):
        rows = slice(slot * row_len, (slot + 1) * row_len)
        gradient = jnp.concatenate(
            [
                received_ref[:, part]
                .astype(jnp.float32)[:, rows]
                .reshape(pieces * row_len, lanes)
                for part in range(parts)
            ],
            axis=1,
        )
        left = jnp.dot(
            left_ref[slot], gradient.astype(jnp.bfloat16), preferred_element_type=jnp.float32
        ).astype(jnp.bfloat16)
        right = jnp.concatenate([right_ref[part, slot] for part in range(parts)], axis=1)
        product = jnp.dot(left, right, preferred_element_type=jnp.float32)
        grad_square = jnp.sum(jnp.square(gradient))
        pre_square = jnp.sum(jnp.square(product))
        factor = jnp.sqrt(jnp.full((1, lanes), grad_square / (pre_square + 1e-06), jnp.float32))
        directions.append(product * factor[:, :1])
    for part in range(parts):
        columns = slice(part * lanes, (part + 1) * lanes)
        out_ref[:, part] = jnp.concatenate(
            [each[:, columns].reshape(pieces, row_len, lanes) for each in directions], axis=1
        ).astype(jnp.bfloat16)


def shards(grads, table, left_root, right_root):
    replicas = lax.axis_size("dp")
    owners_count = lax.axis_size("mp")
    parts = lax.axis_size("inner")
    capacity = left_root.shape[2]
    held = capacity // parts
    _, _, group_len, row_len, col_len = grads.shape
    slot_total = owners_count * capacity
    inner = lax.axis_index("inner")
    params = pltpu.CompilerParams(vmem_limit_bytes=32 * MIB)

    piece = (group_len, row_len, col_len)
    own, *sent = pl.pallas_call(
        spans,
        in_specs=[IN_ANY],
        out_specs=[IN_VMEM] * replicas,
        out_shape=[jax.ShapeDtypeStruct(piece, jnp.bfloat16)] * replicas,
        scratch_shapes=[pltpu.SemaphoreType.DMA((replicas,))],
        compiler_params=pltpu.CompilerParams(vmem_limit_bytes=50 * MIB),
    )(grads[0])
    terms = [own] + [
        lax.ppermute(each, "dp", ring(replicas, step)) for step, each in enumerate(sent, 1)
    ]
    terms[1], right_root = lax.optimization_barrier((terms[1], right_root))
    right = lax.all_to_all(
        right_root[0, 0].reshape(parts, held, *right_root.shape[3:]), "inner", 0, 0, tiled=True
    )

    left = lax.dynamic_slice_in_dim(left_root[0, 0], inner * held, held, 0)

    owner = table[0, :, 0]
    onehot = (owner[:, None] == jnp.arange(owners_count, dtype=jnp.int32)[None, :]).astype(
        jnp.int32
    )
    rank = jnp.sum((jnp.cumsum(onehot, axis=0) - onehot) * onehot, axis=1)
    target = owner * capacity + rank
    sending = (slot_total, row_len, col_len)
    paired = (owners_count * parts, held * row_len, col_len)
    outgoing = pl.pallas_call(
        summed_into_slots,
        in_specs=[IN_SMEM] + [IN_VMEM] * replicas,
        out_specs=IN_VMEM,
        out_shape=jax.ShapeDtypeStruct(sending, jnp.bfloat16),
        compiler_params=params,
    )(target, *terms)
    received = lax.all_to_all(outgoing.reshape(paired), GROUP_AXES, 0, 0, tiled=True)
    shape = (owners_count, parts, held * row_len, col_len)
    direction = pl.pallas_call(
        grafted,
        in_specs=[IN_VMEM] * 3,
        out_specs=IN_VMEM,
        out_shape=jax.ShapeDtypeStruct(shape, jnp.bfloat16),
        compiler_params=params,
    )(received.reshape(shape), left, right)
    returned = lax.all_to_all(direction.reshape(paired), GROUP_AXES, 0, 0, tiled=True)
    result = pl.pallas_call(
        copied,
        in_specs=[IN_SMEM, IN_VMEM],
        out_specs=IN_VMEM,
        out_shape=jax.ShapeDtypeStruct(piece, jnp.bfloat16),
        compiler_params=params,
    )(target, returned.reshape(sending))
    return result[None]


def solution(mesh):
    placed = (
        P("dp", None, None, "mp", "inner"),
        P("dp", None, None),
        P("dp", "mp", None, None, None),
        P("dp", "mp", None, None, "inner"),
    )
    return jax.shard_map(
        shards, mesh=mesh, in_specs=placed, out_specs=P("dp", None, "mp", "inner"), check_vma=False
    )
```
